32 devices in a mesh: groups: 2 (over x), rows: 8 (over z, y), cols: 2 (over core).
Axes of the slice: x: 2, y: 2, z: 4, core: 2. Of those that a mesh axis runs over, the one named last changes fastest.
Arguments:
- rhs_field: bfloat16 [64, 8192], P(None, ('groups', 'rows', 'cols')), parts along dimension 1, may hold values from -6 to 6
- far_left: bfloat16 [32, 64, 64, 256], P(('groups', 'rows', 'cols')), parts along dimension 0, may hold values from -0.09375 to 0.09375
- far_right: bfloat16 [32, 64, 64, 256], P(('groups', 'rows', 'cols')), parts along dimension 0, may hold values from -0.375 to 0.375
- far_rows: int32 [32, 64], P(('groups', 'rows', 'cols')), parts along dimension 0, may hold values from 0 to 15, as said below
- far_cols: int32 [32, 64], P(('groups', 'rows', 'cols')), parts along dimension 0, may hold values from 0 to 15, as said below
- far_ranks: int32 [32, 64], P(('groups', 'rows', 'cols')), parts along dimension 0, may hold values from 8 to 64
- far_counts: int32 [32], P(('groups', 'rows', 'cols')), parts along dimension 0, may hold values from 0 to 64, as said below
- near_blocks: bfloat16 [32, 8, 256, 256], P(('groups', 'rows', 'cols')), parts along dimension 0, may hold values from -0.125 to 0.125
- near_rows: int32 [32, 8], P(('groups', 'rows', 'cols')), parts along dimension 0, may hold values from 0 to 15, as said below
- near_cols: int32 [32, 8], P(('groups', 'rows', 'cols')), parts along dimension 0, may hold values from 0 to 15, as said below
Outputs:
- product: float32 [64, 8192], P(None, ('groups', 'rows', 'cols')), parts along dimension 1
The draws below stay inside these ranges and needn't reach their ends.
There are 2 independent parts, one for each index of `groups`. The reference program is written for one: setup_inputs(seed, part) draws one part's arguments, and reference() takes and returns one part's arrays. A program takes and returns all parts, laid end to end along the dimension named above; each array names one. Nothing has to cross between parts.
Inputs may be any that keep to these rules, and one draw needn't show every extreme that they name: `far_rows`: entry [d, s] divided by 2, rounded down, equals d divided by 2, rounded down. `far_cols`: entry [d, s] modulo 2 equals d modulo 2. `far_counts`: entries d and (d + 8) modulo 16 sum to 64. `near_rows`: entry [d, s] divided by 2, rounded down, equals d divided by 2, rounded down. `near_cols`: entry [d, s] modulo 2 equals d modulo 2, and entry [d, s] divided by 2, rounded down, differs by at most one from d divided by 2, rounded down.
All inputs are finite; a program needn't handle non-finite values.
Results may differ from the reference program's by a relative error of at most 0.0014.
Values may be sent and summed in bfloat16 or wider, within the bound.
A program may use at most 64 MiB of HBM per device.

```python
import jax
import jax.numpy as jnp
from jax import lax

LEAF = 256
RANK = 64
RHS = 64
FAR_SLOTS = 64
NEAR_SLOTS = 8
GRID = 16
ORDER = 4096
N_ROWS = 8
N_COLS = 2


def draw_far_rows(key, part):
    key = jax.random.fold_in(key, 11)
    device = jnp.arange(GRID, dtype=jnp.int32)[:, None]
    within = jax.random.randint(key, (GRID, FAR_SLOTS), 0, N_COLS, dtype=jnp.int32)
    return N_COLS * (device // N_COLS) + within


def draw_far_cols(key, part):
    key = jax.random.fold_in(key, 12)
    device = jnp.arange(GRID, dtype=jnp.int32)[:, None]
    grid_row = jax.random.randint(key, (GRID, FAR_SLOTS), 0, N_ROWS, dtype=jnp.int32)
    return N_COLS * grid_row + device % N_COLS


def draw_far_ranks(key, part):
    key = jax.random.fold_in(key, 13)
    ranks = jax.random.randint(key, (GRID, FAR_SLOTS), RANK // 8, RANK + 1, dtype=jnp.int32)
    return ranks.at[0, 0].set(RANK)


def draw_far_counts(key, part):
    key = jax.random.fold_in(key, 14)
    first_key, second_key = jax.random.split(key)
    paired = GRID // 2
    heavy = jax.random.randint(first_key, (paired,), FAR_SLOTS // 2, FAR_SLOTS + 1, dtype=jnp.int32)
    heavy = heavy.at[0].set(FAR_SLOTS)
    flips = jax.random.randint(second_key, (paired,), 0, 2, dtype=jnp.int32)
    first_half = jnp.where(flips == 1, heavy, FAR_SLOTS - heavy)
    return jnp.concatenate([first_half, FAR_SLOTS - first_half]).astype(jnp.int32)


def draw_near_rows(key, part):
    key = jax.random.fold_in(key, 15)
    device = jnp.arange(GRID, dtype=jnp.int32)[:, None]
    within = jax.random.randint(key, (GRID, NEAR_SLOTS), 0, N_COLS, dtype=jnp.int32)
    return N_COLS * (device // N_COLS) + within


def draw_near_cols(key, part):
    key = jax.random.fold_in(key, 16)
    device = jnp.arange(GRID, dtype=jnp.int32)[:, None]
    offsets = jax.random.randint(key, (GRID, NEAR_SLOTS), -1, 2, dtype=jnp.int32)
    grid_row = jnp.clip(device // N_COLS + offsets, 0, N_ROWS - 1)
    return N_COLS * grid_row + device % N_COLS


def level_of(key, extent, shards, low, top_value):
    loudness, own = 1.0, jax.random.fold_in(key, 6)
    for dim, blocks in shards:
        steps = jnp.exp(jax.random.uniform(jax.random.fold_in(own, dim), (blocks,), jnp.float32, low / len(shards), top_value / len(shards)))
        loudness = loudness * jnp.repeat(steps, extent[dim] // blocks).reshape([-1 if axis == dim else 1 for axis in range(len(extent))])
    return loudness


def noise(rng, shape, scale, most, cuts=(), held_as=jnp.bfloat16):
    drawn = scale * jax.random.normal(rng, shape, jnp.float32)
    if cuts:
        drawn = drawn * level_of(rng, shape, cuts, -0.22, 0.18)
    return jnp.clip(drawn, -most, most).astype(held_as)


def setup_inputs(seed: int = 0, part: int = 0) -> dict:
    seeds = jax.random.split(jax.random.key(seed), 11)
    own_keys = jax.random.split(jax.random.fold_in(seeds[10], part), 11)
    rhs_field = noise(own_keys[0], (RHS, ORDER), 1.0, 6.0, ((1, 16),))
    far_left = noise(own_keys[1], (GRID, FAR_SLOTS, RANK, LEAF), (RANK * FAR_SLOTS) ** -0.5, 0.09375, ((0, 16),))
    far_right = noise(own_keys[2], (GRID, FAR_SLOTS, RANK, LEAF), LEAF ** -0.5, 0.375, ((0, 16),))
    far_rows = draw_far_rows(jax.random.fold_in(jax.random.fold_in(seeds[10], part), 71), part)
    far_cols = draw_far_cols(jax.random.fold_in(jax.random.fold_in(seeds[10], part), 71), part)
    far_ranks = draw_far_ranks(jax.random.fold_in(jax.random.fold_in(seeds[10], part), 71), part)
    far_counts = draw_far_counts(jax.random.fold_in(jax.random.fold_in(seeds[10], part), 71), part)
    near_blocks = noise(own_keys[7], (GRID, NEAR_SLOTS, LEAF, LEAF), (LEAF * NEAR_SLOTS) ** -0.5, 0.125, ((0, 16),))
    near_rows = draw_near_rows(jax.random.fold_in(jax.random.fold_in(seeds[10], part), 71), part)
    near_cols = draw_near_cols(jax.random.fold_in(jax.random.fold_in(seeds[10], part), 71), part)
    return {"rhs_field": rhs_field, "far_left": far_left, "far_right": far_right, "far_rows": far_rows, "far_cols": far_cols, "far_ranks": far_ranks, "far_counts": far_counts, "near_blocks": near_blocks, "near_rows": near_rows, "near_cols": near_cols}


def reference(rhs_field, far_left, far_right, far_rows, far_cols, far_ranks, far_counts, near_blocks, near_rows, near_cols):
    pieces = rhs_field.reshape(RHS, GRID, LEAF).astype(jnp.float32)
    slot_ids = jnp.arange(FAR_SLOTS, dtype=jnp.int32)
    rank_ids = jnp.arange(RANK, dtype=jnp.int32)

    def far_device(running, inputs):
        left, right, rows_here, cols_here, ranks_here, count_here = inputs
        x_pieces = jnp.take(pieces, cols_here.astype(jnp.int32), axis=1)
        scores = jnp.einsum("hsn,skn->hsk", x_pieces, right.astype(jnp.float32))
        kept = (slot_ids < count_here)[:, None] & (rank_ids[None, :] < ranks_here[:, None])
        coefficients = jnp.where(kept[None], scores, jnp.zeros_like(scores)).astype(jnp.bfloat16)
        contribution = jnp.einsum("hsk,skn->hsn", coefficients.astype(jnp.float32), left.astype(jnp.float32))
        return running.at[:, rows_here.astype(jnp.int32), :].add(contribution), None

    def near_device(running, inputs):
        blocks, rows_here, cols_here = inputs
        x_pieces = jnp.take(pieces, cols_here.astype(jnp.int32), axis=1)
        contribution = jnp.einsum("hsn,snm->hsm", x_pieces, blocks.astype(jnp.float32))
        return running.at[:, rows_here.astype(jnp.int32), :].add(contribution), None

    running = jnp.zeros((RHS, GRID, LEAF), jnp.float32)
    running, unused = lax.scan(near_device, running, (near_blocks, near_rows, near_cols))
    running, unused = lax.scan(far_device, running, (far_left, far_right, far_rows, far_cols, far_ranks, far_counts))
    return running.reshape(RHS, GRID * LEAF)
```

```python
import functools

import jax
import jax.numpy as jnp
from jax import lax
from jax.experimental import pallas as pl
from jax.experimental.pallas import tpu as pltpu
from jax.sharding import PartitionSpec as P

MESH = pl.DeviceIdType.MESH


def kernel(
    n_rows,
    n_cols,
    x_ref,
    left_ref,
    right_ref,
    far_rows_ref,
    far_cols_ref,
    far_ranks_ref,
    far_counts_ref,
    near_ref,
    near_rows_ref,
    near_cols_ref,
    out_ref,
    x_all,
    left,
    right,
    near,
    outgoing,
    incoming,
    local_sem,
    send_sem,
    recv_sem,
    pair_sem,
):
    row = lax.axis_index("rows")
    col = lax.axis_index("cols")
    far_slots, rank, leaf = right.shape
    near_slots = near.shape[0]
    rhs = x_ref.shape[0]

    loads = [
        pltpu.make_async_copy(x_ref, x_all.at[row], local_sem.at[0]),
        pltpu.make_async_copy(right_ref.at[0], right, local_sem.at[1]),
        pltpu.make_async_copy(near_ref.at[0], near, local_sem.at[2]),
        pltpu.make_async_copy(left_ref.at[0], left, local_sem.at[3]),
    ]
    for load in loads:
        load.start()

    barrier = pltpu.get_barrier_semaphore()
    for offset in range(1, n_rows):
        peer = lax.rem(row + offset, n_rows)
        pl.semaphore_signal(barrier, inc=1, device_id={"rows": peer}, device_id_type=MESH)
    pl.semaphore_signal(barrier, inc=1, device_id={"cols": 1 - col}, device_id_type=MESH)
    pl.semaphore_wait(barrier, n_rows)

    sends = []
    for offset in range(1, n_rows):
        peer = lax.rem(row + offset, n_rows)
        copy = pltpu.make_async_remote_copy(
            src_ref=x_ref,
            dst_ref=x_all.at[row],
            send_sem=send_sem.at[offset],
            recv_sem=recv_sem.at[offset],
            device_id={"rows": peer},
            device_id_type=MESH,
        )
        copy.start()
        sends.append(copy)
    for offset in range(1, n_rows):
        source = lax.rem(row + n_rows - offset, n_rows)
        pltpu.make_async_remote_copy(
            src_ref=x_ref,
            dst_ref=x_all.at[source],
            send_sem=send_sem.at[offset],
            recv_sem=recv_sem.at[offset],
            device_id={"rows": source},
            device_id_type=MESH,
        ).wait_recv()
    for load in loads:
        load.wait()

    live = far_counts_ref[0]
    acc = jnp.zeros((2 * rhs, leaf), jnp.float32)
    for slot in range(near_slots):
        piece = x_all[near_cols_ref[0, slot] // n_cols]
        mine = near_rows_ref[0, slot] % n_cols == col
        empty = jnp.zeros_like(piece)
        both = jnp.concatenate([jnp.where(mine, piece, empty), jnp.where(mine, empty, piece)], axis=0)
        acc += jnp.dot(both, near[slot], preferred_element_type=jnp.float32)

    width = 2 * rank
    lane = lax.broadcasted_iota(jnp.int32, (rhs, width), 1)
    first = lane < rank
    group = 4
    for start in range(0, far_slots, group):
        halves = []
        for a in range(start, start + group, 2):
            b = a + 1
            pieces = jnp.concatenate(
                [x_all[far_cols_ref[0, a] // n_cols], x_all[far_cols_ref[0, b] // n_cols]], axis=0
            )
            weights = right[a : a + 2].reshape(width, leaf)
            scores = lax.dot_general(
                pieces, weights, (((1,), (1,)), ((), ())), preferred_element_type=jnp.float32
            )
            scores = jnp.where(first, scores[:rhs], scores[rhs:])
            end_a = jnp.where(a < live, far_ranks_ref[0, a], 0)
            end_b = jnp.where(b < live, far_ranks_ref[0, b], 0) + rank
            mine_a = far_rows_ref[0, a] % n_cols == col
            mine_b = far_rows_ref[0, b] % n_cols == col
            own = lane < jnp.where(first, jnp.where(mine_a, end_a, 0), jnp.where(mine_b, end_b, 0))
            other = lane < jnp.where(first, jnp.where(mine_a, 0, end_a), jnp.where(mine_b, 0, end_b))
            halves.append(
                jnp.concatenate(
                    [jnp.where(own, scores, 0.0), jnp.where(other, scores, 0.0)], axis=0
                ).astype(jnp.bfloat16)
            )
        coefficients = jnp.concatenate(halves, axis=1)
        acc += jnp.dot(
            coefficients,
            left[start : start + group].reshape(group * rank, leaf),
            preferred_element_type=jnp.float32,
        )

    outgoing[...] = acc[rhs:]
    exchange = pltpu.make_async_remote_copy(
        src_ref=outgoing,
        dst_ref=incoming,
        send_sem=pair_sem.at[0],
        recv_sem=pair_sem.at[1],
        device_id={"cols": 1 - col},
        device_id_type=MESH,
    )
    exchange.start()
    for copy in sends:
        copy.wait_send()
    exchange.wait()
    out_ref[...] = acc[:rhs] + incoming[...]


def on_device(
    n_rows,
    n_cols,
    rhs_field,
    far_left,
    far_right,
    far_rows,
    far_cols,
    far_ranks,
    far_counts,
    near_blocks,
    near_rows,
    near_cols,
):
    rhs, leaf = rhs_field.shape
    anywhere = pl.BlockSpec(memory_space=pl.ANY)
    scalars = pl.BlockSpec(memory_space=pltpu.SMEM)
    return pl.pallas_call(
        functools.partial(kernel, n_rows, n_cols),
        out_shape=jax.ShapeDtypeStruct((rhs, leaf), jnp.float32),
        in_specs=[
            anywhere,
            anywhere,
            anywhere,
            scalars,
            scalars,
            scalars,
            scalars,
            anywhere,
            scalars,
            scalars,
        ],
        out_specs=pl.BlockSpec(memory_space=pltpu.VMEM),
        scratch_shapes=[
            pltpu.VMEM((n_rows, rhs, leaf), jnp.bfloat16),
            pltpu.VMEM(far_left.shape[1:], jnp.bfloat16),
            pltpu.VMEM(far_right.shape[1:], jnp.bfloat16),
            pltpu.VMEM(near_blocks.shape[1:], jnp.bfloat16),
            pltpu.VMEM((rhs, leaf), jnp.float32),
            pltpu.VMEM((rhs, leaf), jnp.float32),
            pltpu.SemaphoreType.DMA((4,)),
            pltpu.SemaphoreType.DMA((n_rows,)),
            pltpu.SemaphoreType.DMA((n_rows,)),
            pltpu.SemaphoreType.DMA((2,)),
        ],
        compiler_params=pltpu.CompilerParams(
            collective_id=0, has_side_effects=True, vmem_limit_bytes=32 * 1024 * 1024
        ),
    )(
        rhs_field,
        far_left,
        far_right,
        far_rows,
        far_cols,
        far_ranks,
        far_counts,
        near_blocks,
        near_rows,
        near_cols,
    )


def solution(mesh):
    split = ("groups", "rows", "cols")
    placed = (
        P(None, split),
        P(split, None, None, None),
        P(split, None, None, None),
        P(split, None),
        P(split, None),
        P(split, None),
        P(split),
        P(split, None, None, None),
        P(split, None),
        P(split, None),
    )
    return jax.shard_map(
        functools.partial(on_device, mesh.shape["rows"], mesh.shape["cols"]),
        mesh=mesh,
        in_specs=placed,
        out_specs=P(None, split),
        check_vma=False,
    )
```

```python
import functools

import jax
import jax.numpy as jnp
from jax import lax
from jax.experimental import pallas as pl
from jax.experimental.pallas import tpu as pltpu
from jax.sharding import PartitionSpec as P

MESH = pl.DeviceIdType.MESH


def kernel(
    n_rows,
    n_cols,
    x_ref,
    left_ref,
    right_ref,
    far_rows_ref,
    far_cols_ref,
    far_ranks_ref,
    far_counts_ref,
    near_ref,
    near_rows_ref,
    near_cols_ref,
    out_ref,
    x_all,
    left,
    right,
    near,
    outgoing,
    incoming,
    far_rows,
    far_cols,
    far_ranks,
    far_counts,
    near_rows,
    near_cols,
    local_sem,
    small_sem,
    send_sem,
    recv_sem,
    pair_sem,
):
    row = lax.axis_index("rows")
    col = lax.axis_index("cols")
    far_slots, rank, leaf = right.shape
    near_slots = near.shape[0]
    rhs = x_ref.shape[0]

    loads = [
        pltpu.make_async_copy(x_ref, x_all.at[row], local_sem.at[0]),
        pltpu.make_async_copy(right_ref.at[0], right, local_sem.at[1]),
        pltpu.make_async_copy(near_ref.at[0], near, local_sem.at[2]),
        pltpu.make_async_copy(left_ref.at[0], left, local_sem.at[3]),
    ]
    small = [
        pltpu.make_async_copy(source, target, small_sem.at[place])
        for place, (source, target) in enumerate(
            [
                (far_rows_ref, far_rows),
                (far_cols_ref, far_cols),
                (far_ranks_ref, far_ranks),
                (far_counts_ref, far_counts),
                (near_rows_ref, near_rows),
                (near_cols_ref, near_cols),
            ]
        )
    ]
    loads = small + loads
    for load in loads:
        load.start()

    barrier = pltpu.get_barrier_semaphore()
    for offset in range(1, n_rows):
        peer = lax.rem(row + offset, n_rows)
        pl.semaphore_signal(barrier, inc=1, device_id={"rows": peer}, device_id_type=MESH)
    pl.semaphore_signal(barrier, inc=1, device_id={"cols": 1 - col}, device_id_type=MESH)
    pl.semaphore_wait(barrier, n_rows)

    sends = []
    for offset in range(1, n_rows):
        peer = lax.rem(row + offset, n_rows)
        copy = pltpu.make_async_remote_copy(
            src_ref=x_ref,
            dst_ref=x_all.at[row],
            send_sem=send_sem.at[offset],
            recv_sem=recv_sem.at[offset],
            device_id={"rows": peer},
            device_id_type=MESH,
        )
        copy.start()
        sends.append(copy)
    for offset in range(1, n_rows):
        source = lax.rem(row + n_rows - offset, n_rows)
        pltpu.make_async_remote_copy(
            src_ref=x_ref,
            dst_ref=x_all.at[source],
            send_sem=send_sem.at[offset],
            recv_sem=recv_sem.at[offset],
            device_id={"rows": source},
            device_id_type=MESH,
        ).wait_recv()
    for load in loads:
        load.wait()

    live = far_counts[0, 0]
    acc = jnp.zeros((2 * rhs, leaf), jnp.float32)
    for slot in range(near_slots):
        piece = x_all[near_cols[0, slot] // n_cols]
        mine = near_rows[0, slot] % n_cols == col
        empty = jnp.zeros_like(piece)
        both = jnp.concatenate([jnp.where(mine, piece, empty), jnp.where(mine, empty, piece)], axis=0)
        acc += jnp.dot(both, near[slot], preferred_element_type=jnp.float32)

    width = 2 * rank
    lane = lax.broadcasted_iota(jnp.int32, (rhs, width), 1)
    first = lane < rank
    group = 4
    for start in range(0, far_slots, group):
        halves = []
        for a in range(start, start + group, 2):
            b = a + 1
            pieces = jnp.concatenate(
                [x_all[far_cols[0, a] // n_cols], x_all[far_cols[0, b] // n_cols]], axis=0
            )
            weights = right[a : a + 2].reshape(width, leaf)
            scores = lax.dot_general(
                pieces, weights, (((1,), (1,)), ((), ())), preferred_element_type=jnp.float32
            )
            scores = jnp.where(first, scores[:rhs], scores[rhs:])
            end_a = jnp.where(a < live, far_ranks[0, a], 0)
            end_b = jnp.where(b < live, far_ranks[0, b], 0) + rank
            mine_a = far_rows[0, a] % n_cols == col
            mine_b = far_rows[0, b] % n_cols == col
            own = lane < jnp.where(first, jnp.where(mine_a, end_a, 0), jnp.where(mine_b, end_b, 0))
            other = lane < jnp.where(first, jnp.where(mine_a, 0, end_a), jnp.where(mine_b, 0, end_b))
            halves.append(
                jnp.concatenate(
                    [jnp.where(own, scores, 0.0), jnp.where(other, scores, 0.0)], axis=0
                ).astype(jnp.bfloat16)
            )
        coefficients = jnp.concatenate(halves, axis=1)
        acc += jnp.dot(
            coefficients,
            left[start : start + group].reshape(group * rank, leaf),
            preferred_element_type=jnp.float32,
        )

    outgoing[...] = acc[rhs:]
    exchange = pltpu.make_async_remote_copy(
        src_ref=outgoing,
        dst_ref=incoming,
        send_sem=pair_sem.at[0],
        recv_sem=pair_sem.at[1],
        device_id={"cols": 1 - col},
        device_id_type=MESH,
    )
    exchange.start()
    for copy in sends:
        copy.wait_send()
    exchange.wait()
    out_ref[...] = acc[:rhs] + incoming[...]


def on_device(
    n_rows,
    n_cols,
    rhs_field,
    far_left,
    far_right,
    far_rows,
    far_cols,
    far_ranks,
    far_counts,
    near_blocks,
    near_rows,
    near_cols,
):
    rhs, leaf = rhs_field.shape
    in_hbm = pl.BlockSpec(memory_space=pltpu.HBM)
    return pl.pallas_call(
        functools.partial(kernel, n_rows, n_cols),
        out_shape=jax.ShapeDtypeStruct((rhs, leaf), jnp.float32),
        in_specs=[in_hbm] * 10,
        out_specs=pl.BlockSpec(memory_space=pltpu.VMEM),
        scratch_shapes=[
            pltpu.VMEM((n_rows, rhs, leaf), jnp.bfloat16),
            pltpu.VMEM(far_left.shape[1:], jnp.bfloat16),
            pltpu.VMEM(far_right.shape[1:], jnp.bfloat16),
            pltpu.VMEM(near_blocks.shape[1:], jnp.bfloat16),
            pltpu.VMEM((rhs, leaf), jnp.float32),
            pltpu.VMEM((rhs, leaf), jnp.float32),
            pltpu.SMEM(far_rows.shape, jnp.int32),
            pltpu.SMEM(far_cols.shape, jnp.int32),
            pltpu.SMEM(far_ranks.shape, jnp.int32),
            pltpu.SMEM((1, 1), jnp.int32),
            pltpu.SMEM(near_rows.shape, jnp.int32),
            pltpu.SMEM(near_cols.shape, jnp.int32),
            pltpu.SemaphoreType.DMA((4,)),
            pltpu.SemaphoreType.DMA((6,)),
            pltpu.SemaphoreType.DMA((n_rows,)),
            pltpu.SemaphoreType.DMA((n_rows,)),
            pltpu.SemaphoreType.DMA((2,)),
        ],
        compiler_params=pltpu.CompilerParams(
            collective_id=0, has_side_effects=True, vmem_limit_bytes=60 * 1024 * 1024
        ),
    )(
        rhs_field,
        far_left,
        far_right,
        far_rows,
        far_cols,
        far_ranks,
        far_counts.reshape(1, 1),
        near_blocks,
        near_rows,
        near_cols,
    )


def solution(mesh):
    split = ("groups", "rows", "cols")
    placed = (
        P(None, split),
        P(split, None, None, None),
        P(split, None, None, None),
        P(split, None),
        P(split, None),
        P(split, None),
        P(split),
        P(split, None, None, None),
        P(split, None),
        P(split, None),
    )
    return jax.shard_map(
        functools.partial(on_device, mesh.shape["rows"], mesh.shape["cols"]),
        mesh=mesh,
        in_specs=placed,
        out_specs=P(None, split),
        check_vma=False,
    )
```

```python
import functools

import jax
import jax.numpy as jnp
from jax import lax
from jax.experimental import pallas as pl
from jax.experimental.pallas import tpu as pltpu
from jax.sharding import PartitionSpec as P

MESH = pl.DeviceIdType.MESH


def kernel(
    n_rows,
    n_cols,
    x_ref,
    left_ref,
    right_ref,
    far_rows_ref,
    far_cols_ref,
    far_ranks_ref,
    far_counts_ref,
    near_ref,
    near_rows_ref,
    near_cols_ref,
    out_ref,
    x_all,
    left,
    right,
    near,
    outgoing,
    incoming,
    far_rows,
    far_cols,
    far_ranks,
    near_rows,
    near_cols,
    local_sem,
    small_sem,
    send_sem,
    recv_sem,
    pair_sem,
):
    row = lax.axis_index("rows")
    col = lax.axis_index("cols")
    far_slots, rank, leaf = right.shape
    near_slots = near.shape[0]
    rhs = x_ref.shape[0]

    loads = [
        pltpu.make_async_copy(x_ref, x_all.at[row], local_sem.at[0]),
        pltpu.make_async_copy(right_ref.at[0], right, local_sem.at[1]),
        pltpu.make_async_copy(near_ref.at[0], near, local_sem.at[2]),
        pltpu.make_async_copy(left_ref.at[0], left, local_sem.at[3]),
    ]
    small = [
        pltpu.make_async_copy(source, target, small_sem.at[place])
        for place, (source, target) in enumerate(
            [
                (far_rows_ref, far_rows),
                (far_cols_ref, far_cols),
                (far_ranks_ref, far_ranks),
                (near_rows_ref, near_rows),
                (near_cols_ref, near_cols),
            ]
        )
    ]
    loads = small + loads
    for load in loads:
        load.start()

    barrier = pltpu.get_barrier_semaphore()
    for offset in range(1, n_rows):
        peer = lax.rem(row + offset, n_rows)
        pl.semaphore_signal(barrier, inc=1, device_id={"rows": peer}, device_id_type=MESH)
    pl.semaphore_signal(barrier, inc=1, device_id={"cols": 1 - col}, device_id_type=MESH)
    pl.semaphore_wait(barrier, n_rows)

    sends = []
    for offset in range(1, n_rows):
        peer = lax.rem(row + offset, n_rows)
        copy = pltpu.make_async_remote_copy(
            src_ref=x_ref,
            dst_ref=x_all.at[row],
            send_sem=send_sem.at[offset],
            recv_sem=recv_sem.at[offset],
            device_id={"rows": peer},
            device_id_type=MESH,
        )
        copy.start()
        sends.append(copy)
    for offset in range(1, n_rows):
        source = lax.rem(row + n_rows - offset, n_rows)
        pltpu.make_async_remote_copy(
            src_ref=x_ref,
            dst_ref=x_all.at[source],
            send_sem=send_sem.at[offset],
            recv_sem=recv_sem.at[offset],
            device_id={"rows": source},
            device_id_type=MESH,
        ).wait_recv()
    for load in loads:
        load.wait()

    live = far_counts_ref[0]
    acc = jnp.zeros((2 * rhs, leaf), jnp.float32)
    for slot in range(near_slots):
        piece = x_all[near_cols[0, slot] // n_cols]
        mine = near_rows[0, slot] % n_cols == col
        empty = jnp.zeros_like(piece)
        both = jnp.concatenate([jnp.where(mine, piece, empty), jnp.where(mine, empty, piece)], axis=0)
        acc += jnp.dot(both, near[slot], preferred_element_type=jnp.float32)

    width = 2 * rank
    lane = lax.broadcasted_iota(jnp.int32, (rhs, width), 1)
    first = lane < rank
    group = 4
    for start in range(0, far_slots, group):
        halves = []
        for a in range(start, start + group, 2):
            b = a + 1
            pieces = jnp.concatenate(
                [x_all[far_cols[0, a] // n_cols], x_all[far_cols[0, b] // n_cols]], axis=0
            )
            weights = right[a : a + 2].reshape(width, leaf)
            scores = lax.dot_general(
                pieces, weights, (((1,), (1,)), ((), ())), preferred_element_type=jnp.float32
            )
            scores = jnp.where(first, scores[:rhs], scores[rhs:])
            end_a = jnp.where(a < live, far_ranks[0, a], 0)
            end_b = jnp.where(b < live, far_ranks[0, b], 0) + rank
            mine_a = far_rows[0, a] % n_cols == col
            mine_b = far_rows[0, b] % n_cols == col
            own = lane < jnp.where(first, jnp.where(mine_a, end_a, 0), jnp.where(mine_b, end_b, 0))
            other = lane < jnp.where(first, jnp.where(mine_a, 0, end_a), jnp.where(mine_b, 0, end_b))
            halves.append(
                jnp.concatenate(
                    [jnp.where(own, scores, 0.0), jnp.where(other, scores, 0.0)], axis=0
                ).astype(jnp.bfloat16)
            )
        coefficients = jnp.concatenate(halves, axis=1)
        acc += jnp.dot(
            coefficients,
            left[start : start + group].reshape(group * rank, leaf),
            preferred_element_type=jnp.float32,
        )

    outgoing[...] = acc[rhs:]
    exchange = pltpu.make_async_remote_copy(
        src_ref=outgoing,
        dst_ref=incoming,
        send_sem=pair_sem.at[0],
        recv_sem=pair_sem.at[1],
        device_id={"cols": 1 - col},
        device_id_type=MESH,
    )
    exchange.start()
    for copy in sends:
        copy.wait_send()
    exchange.wait()
    out_ref[...] = acc[:rhs] + incoming[...]


def on_device(
    n_rows,
    n_cols,
    rhs_field,
    far_left,
    far_right,
    far_rows,
    far_cols,
    far_ranks,
    far_counts,
    near_blocks,
    near_rows,
    near_cols,
):
    rhs, leaf = rhs_field.shape
    def stay(operand):
        return pltpu.with_memory_space_constraint(operand, pltpu.HBM)

    operands = [
        stay(rhs_field),
        stay(far_left),
        stay(far_right),
        stay(far_rows),
        stay(far_cols),
        stay(far_ranks),
        far_counts,
        stay(near_blocks),
        stay(near_rows),
        stay(near_cols),
    ]
    in_hbm = pl.BlockSpec(memory_space=pltpu.HBM)
    return pl.pallas_call(
        functools.partial(kernel, n_rows, n_cols),
        out_shape=jax.ShapeDtypeStruct((rhs, leaf), jnp.float32),
        in_specs=[in_hbm] * 6 + [pl.BlockSpec(memory_space=pltpu.SMEM)] + [in_hbm] * 3,
        out_specs=pl.BlockSpec(memory_space=pltpu.VMEM),
        scratch_shapes=[
            pltpu.VMEM((n_rows, rhs, leaf), jnp.bfloat16),
            pltpu.VMEM(far_left.shape[1:], jnp.bfloat16),
            pltpu.VMEM(far_right.shape[1:], jnp.bfloat16),
            pltpu.VMEM(near_blocks.shape[1:], jnp.bfloat16),
            pltpu.VMEM((rhs, leaf), jnp.float32),
            pltpu.VMEM((rhs, leaf), jnp.float32),
            pltpu.SMEM(far_rows.shape, jnp.int32),
            pltpu.SMEM(far_cols.shape, jnp.int32),
            pltpu.SMEM(far_ranks.shape, jnp.int32),
            pltpu.SMEM(near_rows.shape, jnp.int32),
            pltpu.SMEM(near_cols.shape, jnp.int32),
            pltpu.SemaphoreType.DMA((4,)),
            pltpu.SemaphoreType.DMA((5,)),
            pltpu.SemaphoreType.DMA((n_rows,)),
            pltpu.SemaphoreType.DMA((n_rows,)),
            pltpu.SemaphoreType.DMA((2,)),
        ],
        compiler_params=pltpu.CompilerParams(
            collective_id=0, has_side_effects=True, vmem_limit_bytes=32 * 1024 * 1024
        ),
    )(*operands)


def solution(mesh):
    split = ("groups", "rows", "cols")
    placed = (
        P(None, split),
        P(split, None, None, None),
        P(split, None, None, None),
        P(split, None),
        P(split, None),
        P(split, None),
        P(split),
        P(split, None, None, None),
        P(split, None),
        P(split, None),
    )
    return jax.shard_map(
        functools.partial(on_device, mesh.shape["rows"], mesh.shape["cols"]),
        mesh=mesh,
        in_specs=placed,
        out_specs=P(None, split),
        check_vma=False,
    )
```

```python
import functools

import jax
import jax.numpy as jnp
from jax import lax
from jax.experimental import pallas as pl
from jax.experimental.pallas import tpu as pltpu
from jax.sharding import PartitionSpec as P

MESH = pl.DeviceIdType.MESH


def kernel(
    n_rows,
    n_cols,
    x_ref,
    left_ref,
    right_ref,
    far_rows_ref,
    far_cols_ref,
    far_ranks_ref,
    far_counts_ref,
    near_ref,
    near_rows_ref,
    near_cols_ref,
    out_ref,
    x_all,
    left,
    right,
    near,
    outgoing,
    incoming,
    far_rows,
    far_cols,
    far_ranks,
    near_rows,
    near_cols,
    here_sem,
    local_sem,
    small_sem,
    send_sem,
    recv_sem,
    pair_sem,
):
    row = lax.axis_index("rows")
    col = lax.axis_index("cols")
    far_slots, rank, leaf = right.shape
    near_slots = near.shape[0]
    pieces, _, rhs, _ = x_all.shape

    small = [
        pltpu.make_async_copy(source, target, small_sem.at[place])
        for place, (source, target) in enumerate(
            [
                (far_rows_ref, far_rows),
                (far_cols_ref, far_cols),
                (far_ranks_ref, far_ranks),
                (near_rows_ref, near_rows),
                (near_cols_ref, near_cols),
            ]
        )
    ]
    large = [
        pltpu.make_async_copy(right_ref.at[0], right, local_sem.at[0]),
        pltpu.make_async_copy(near_ref.at[0], near, local_sem.at[1]),
        pltpu.make_async_copy(left_ref.at[0], left, local_sem.at[2]),
    ]
    here = [
        pltpu.make_async_copy(
            x_ref.at[piece * rhs : (piece + 1) * rhs], x_all.at[piece, row], here_sem.at[piece]
        )
        for piece in range(pieces)
    ]
    loads = here + small + large
    for load in loads:
        load.start()

    peers = [
        (lax.rem(row + offset, n_rows), lax.rem(row + n_rows - offset, n_rows))
        for offset in range(1, n_rows)
    ]
    barrier = pltpu.get_barrier_semaphore()
    for target, _ in peers:
        pl.semaphore_signal(barrier, inc=1, device_id={"rows": target}, device_id_type=MESH)
    pl.semaphore_signal(barrier, inc=1, device_id={"cols": 1 - col}, device_id_type=MESH)
    pl.semaphore_wait(barrier, n_rows)

    def push(piece, number, origin, target):
        return pltpu.make_async_remote_copy(
            src_ref=x_ref.at[piece * rhs : (piece + 1) * rhs],
            dst_ref=x_all.at[piece, origin],
            send_sem=send_sem.at[piece, number],
            recv_sem=recv_sem.at[piece, number],
            device_id={"rows": target},
            device_id_type=MESH,
        )

    sends = []
    for piece in range(pieces):
        for number, (target, _) in enumerate(peers):
            sends.append(push(piece, number, row, target))
            sends[-1].start()
    for load in loads:
        load.wait()

    live = far_counts_ref[0]
    width = 2 * rank
    lane = lax.broadcasted_iota(jnp.int32, (1, width), 1)
    first = lane < rank
    exchanges = []
    for piece in range(pieces):
        for number, (target, source) in enumerate(peers):
            push(piece, number, source, target).wait_recv()

        acc = jnp.zeros((2 * rhs, leaf), jnp.float32)
        for slot in range(near_slots):
            block = x_all[piece, near_cols[0, slot] // n_cols]
            mine = near_rows[0, slot] % n_cols == col
            empty = jnp.zeros_like(block)
            both = jnp.concatenate(
                [jnp.where(mine, block, empty), jnp.where(mine, empty, block)], axis=0
            )
            acc += jnp.dot(both, near[slot], preferred_element_type=jnp.float32)

        coefficients = []
        for start in range(0, far_slots, 2):
            slots = range(start, start + 2)
            blocks = jnp.concatenate(
                [x_all[piece, far_cols[0, slot] // n_cols] for slot in slots], axis=0
            )
            scores = lax.dot_general(
                blocks,
                right[start : start + 2].reshape(2 * rank, leaf),
                (((1,), (1,)), ((), ())),
                preferred_element_type=jnp.float32,
            )
            for place in range(0, 2, 2):
                a, b = start + place, start + place + 1
                columns = scores[:, place * rank : (place + 2) * rank]
                kept = jnp.where(
                    first,
                    columns[place * rhs : (place + 1) * rhs],
                    columns[(place + 1) * rhs : (place + 2) * rhs],
                )
                end_a = jnp.where(a < live, far_ranks[0, a], 0)
                end_b = jnp.where(b < live, far_ranks[0, b], 0) + rank
                mine_a = far_rows[0, a] % n_cols == col
                mine_b = far_rows[0, b] % n_cols == col
                own = lane < jnp.where(
                    first, jnp.where(mine_a, end_a, 0), jnp.where(mine_b, end_b, 0)
                )
                other = lane < jnp.where(
                    first, jnp.where(mine_a, 0, end_a), jnp.where(mine_b, 0, end_b)
                )
                coefficients.append(
                    jnp.concatenate(
                        [jnp.where(own, kept, 0.0), jnp.where(other, kept, 0.0)], axis=0
                    ).astype(jnp.bfloat16)
                )
        acc += jnp.dot(
            jnp.concatenate(coefficients, axis=1),
            left[...].reshape(far_slots * rank, leaf),
            preferred_element_type=jnp.float32,
        )

        outgoing[piece] = acc[rhs:]
        exchanges.append(
            pltpu.make_async_remote_copy(
                src_ref=outgoing.at[piece],
                dst_ref=incoming.at[piece],
                send_sem=pair_sem.at[0, piece],
                recv_sem=pair_sem.at[1, piece],
                device_id={"cols": 1 - col},
                device_id_type=MESH,
            )
        )
        exchanges[-1].start()
        out_ref[piece * rhs : (piece + 1) * rhs] = acc[:rhs]

    for copy in sends:
        copy.wait_send()
    for piece in range(pieces):
        exchanges[piece].wait()
        out_ref[piece * rhs : (piece + 1) * rhs] += incoming[piece]


def on_device(
    n_rows,
    n_cols,
    rhs_field,
    far_left,
    far_right,
    far_rows,
    far_cols,
    far_ranks,
    far_counts,
    near_blocks,
    near_rows,
    near_cols,
):
    rhs, leaf = rhs_field.shape
    pieces = 1
    def stay(operand):
        return pltpu.with_memory_space_constraint(operand, pltpu.HBM)

    operands = [
        stay(rhs_field),
        stay(far_left),
        stay(far_right),
        stay(far_rows),
        stay(far_cols),
        stay(far_ranks),
        far_counts,
        stay(near_blocks),
        stay(near_rows),
        stay(near_cols),
    ]
    in_hbm = pl.BlockSpec(memory_space=pltpu.HBM)
    return pl.pallas_call(
        functools.partial(kernel, n_rows, n_cols),
        out_shape=jax.ShapeDtypeStruct((rhs, leaf), jnp.float32),
        in_specs=[in_hbm] * 6 + [pl.BlockSpec(memory_space=pltpu.SMEM)] + [in_hbm] * 3,
        out_specs=pl.BlockSpec(memory_space=pltpu.VMEM),
        scratch_shapes=[
            pltpu.VMEM((pieces, n_rows, rhs // pieces, leaf), jnp.bfloat16),
            pltpu.VMEM(far_left.shape[1:], jnp.bfloat16),
            pltpu.VMEM(far_right.shape[1:], jnp.bfloat16),
            pltpu.VMEM(near_blocks.shape[1:], jnp.bfloat16),
            pltpu.VMEM((pieces, rhs // pieces, leaf), jnp.float32),
            pltpu.VMEM((pieces, rhs // pieces, leaf), jnp.float32),
            pltpu.SMEM(far_rows.shape, jnp.int32),
            pltpu.SMEM(far_cols.shape, jnp.int32),
            pltpu.SMEM(far_ranks.shape, jnp.int32),
            pltpu.SMEM(near_rows.shape, jnp.int32),
            pltpu.SMEM(near_cols.shape, jnp.int32),
            pltpu.SemaphoreType.DMA((pieces,)),
            pltpu.SemaphoreType.DMA((3,)),
            pltpu.SemaphoreType.DMA((5,)),
            pltpu.SemaphoreType.DMA((pieces, n_rows)),
            pltpu.SemaphoreType.DMA((pieces, n_rows)),
            pltpu.SemaphoreType.DMA((2, pieces)),
        ],
        compiler_params=pltpu.CompilerParams(
            collective_id=0, has_side_effects=True, vmem_limit_bytes=32 * 1024 * 1024
        ),
    )(*operands)


def solution(mesh):
    split = ("groups", "rows", "cols")
    placed = (
        P(None, split),
        P(split, None, None, None),
        P(split, None, None, None),
        P(split, None),
        P(split, None),
        P(split, None),
        P(split),
        P(split, None, None, None),
        P(split, None),
        P(split, None),
    )
    return jax.shard_map(
        functools.partial(on_device, mesh.shape["rows"], mesh.shape["cols"]),
        mesh=mesh,
        in_specs=placed,
        out_specs=P(None, split),
        check_vma=False,
    )
```

```python
import functools

import jax
import jax.numpy as jnp
from jax import lax
from jax.experimental import pallas as pl
from jax.experimental.pallas import tpu as pltpu
from jax.sharding import PartitionSpec as P

MESH = pl.DeviceIdType.MESH


def kernel(
    n_rows,
    n_cols,
    x_ref,
    left_ref,
    right_ref,
    far_rows_ref,
    far_cols_ref,
    far_ranks_ref,
    far_counts_ref,
    near_ref,
    near_rows_ref,
    near_cols_ref,
    out_ref,
    x_all,
    left,
    right,
    near,
    outgoing,
    incoming,
    far_rows,
    far_cols,
    far_ranks,
    near_rows,
    near_cols,
    here_sem,
    local_sem,
    small_sem,
    send_sem,
    recv_sem,
    pair_sem,
):
    row = lax.axis_index("rows")
    col = lax.axis_index("cols")
    far_slots, rank, leaf = right.shape
    near_slots = near.shape[0]
    pieces, _, rhs, _ = x_all.shape

    small = [
        pltpu.make_async_copy(source, target, small_sem.at[place])
        for place, (source, target) in enumerate(
            [
                (far_rows_ref, far_rows),
                (far_cols_ref, far_cols),
                (far_ranks_ref, far_ranks),
                (near_rows_ref, near_rows),
                (near_cols_ref, near_cols),
            ]
        )
    ]
    large = [
        pltpu.make_async_copy(right_ref.at[0], right, local_sem.at[0]),
        pltpu.make_async_copy(near_ref.at[0], near, local_sem.at[1]),
        pltpu.make_async_copy(left_ref.at[0], left, local_sem.at[2]),
    ]
    here = [
        pltpu.make_async_copy(
            x_ref.at[piece * rhs : (piece + 1) * rhs], x_all.at[piece, row], here_sem.at[piece]
        )
        for piece in range(pieces)
    ]
    loads = here + small + large
    for load in loads:
        load.start()

    peers = [
        (lax.rem(row + offset, n_rows), lax.rem(row + n_rows - offset, n_rows))
        for offset in range(1, n_rows)
    ]
    barrier = pltpu.get_barrier_semaphore()
    for target, _ in peers:
        pl.semaphore_signal(barrier, inc=1, device_id={"rows": target}, device_id_type=MESH)
    pl.semaphore_signal(barrier, inc=1, device_id={"cols": 1 - col}, device_id_type=MESH)
    pl.semaphore_wait(barrier, n_rows)

    def push(piece, number, origin, target):
        return pltpu.make_async_remote_copy(
            src_ref=x_ref.at[piece * rhs : (piece + 1) * rhs],
            dst_ref=x_all.at[piece, origin],
            send_sem=send_sem.at[piece, number],
            recv_sem=recv_sem.at[piece, number],
            device_id={"rows": target},
            device_id_type=MESH,
        )

    sends = []
    for piece in range(pieces):
        for number, (target, _) in enumerate(peers):
            sends.append(push(piece, number, row, target))
            sends[-1].start()
    for load in loads:
        load.wait()

    live = far_counts_ref[0]
    width = 2 * rank
    lane = lax.broadcasted_iota(jnp.int32, (1, width), 1)
    first = lane < rank
    exchanges = []
    for piece in range(pieces):
        arrivals = [
            push(piece, number, source, target) for number, (target, source) in enumerate(peers)
        ]
        arrivals[0].wait_recv()
        arrivals[-1].wait_recv()

        acc = jnp.zeros((2 * rhs, leaf), jnp.float32)
        below, above = lax.rem(row + n_rows - 1, n_rows), lax.rem(row + 1, n_rows)
        beside = [x_all[piece, below], x_all[piece, row], x_all[piece, above]]
        for slot in range(near_slots):
            key = near_cols[0, slot] // n_cols
            block = jnp.where(key < row, beside[0], jnp.where(key == row, beside[1], beside[2]))
            mine = near_rows[0, slot] % n_cols == col
            empty = jnp.zeros_like(block)
            both = jnp.concatenate(
                [jnp.where(mine, block, empty), jnp.where(mine, empty, block)], axis=0
            )
            acc += jnp.dot(both, near[slot], preferred_element_type=jnp.float32)

        for arrival in arrivals[1:-1]:
            arrival.wait_recv()

        coefficients = []
        for start in range(0, far_slots, 2):
            slots = range(start, start + 2)
            blocks = jnp.concatenate(
                [x_all[piece, far_cols[0, slot] // n_cols] for slot in slots], axis=0
            )
            scores = lax.dot_general(
                blocks,
                right[start : start + 2].reshape(2 * rank, leaf),
                (((1,), (1,)), ((), ())),
                preferred_element_type=jnp.float32,
            )
            for place in range(0, 2, 2):
                a, b = start + place, start + place + 1
                columns = scores[:, place * rank : (place + 2) * rank]
                kept = jnp.where(
                    first,
                    columns[place * rhs : (place + 1) * rhs],
                    columns[(place + 1) * rhs : (place + 2) * rhs],
                )
                end_a = jnp.where(a < live, far_ranks[0, a], 0)
                end_b = jnp.where(b < live, far_ranks[0, b], 0) + rank
                mine_a = far_rows[0, a] % n_cols == col
                mine_b = far_rows[0, b] % n_cols == col
                own = lane < jnp.where(
                    first, jnp.where(mine_a, end_a, 0), jnp.where(mine_b, end_b, 0)
                )
                other = lane < jnp.where(
                    first, jnp.where(mine_a, 0, end_a), jnp.where(mine_b, 0, end_b)
                )
                coefficients.append(
                    jnp.concatenate(
                        [jnp.where(own, kept, 0.0), jnp.where(other, kept, 0.0)], axis=0
                    ).astype(jnp.bfloat16)
                )
        acc += jnp.dot(
            jnp.concatenate(coefficients, axis=1),
            left[...].reshape(far_slots * rank, leaf),
            preferred_element_type=jnp.float32,
        )

        outgoing[piece] = acc[rhs:]
        exchanges.append(
            pltpu.make_async_remote_copy(
                src_ref=outgoing.at[piece],
                dst_ref=incoming.at[piece],
                send_sem=pair_sem.at[0, piece],
                recv_sem=pair_sem.at[1, piece],
                device_id={"cols": 1 - col},
                device_id_type=MESH,
            )
        )
        exchanges[-1].start()
        out_ref[piece * rhs : (piece + 1) * rhs] = acc[:rhs]

    for copy in sends:
        copy.wait_send()
    for piece in range(pieces):
        exchanges[piece].wait()
        out_ref[piece * rhs : (piece + 1) * rhs] += incoming[piece]


def on_device(
    n_rows,
    n_cols,
    rhs_field,
    far_left,
    far_right,
    far_rows,
    far_cols,
    far_ranks,
    far_counts,
    near_blocks,
    near_rows,
    near_cols,
):
    rhs, leaf = rhs_field.shape
    pieces = 1
    def stay(operand):
        return pltpu.with_memory_space_constraint(operand, pltpu.HBM)

    operands = [
        stay(rhs_field),
        stay(far_left),
        stay(far_right),
        stay(far_rows),
        stay(far_cols),
        stay(far_ranks),
        far_counts,
        stay(near_blocks),
        stay(near_rows),
        stay(near_cols),
    ]
    in_hbm = pl.BlockSpec(memory_space=pltpu.HBM)
    return pl.pallas_call(
        functools.partial(kernel, n_rows, n_cols),
        out_shape=jax.ShapeDtypeStruct((rhs, leaf), jnp.float32),
        in_specs=[in_hbm] * 6 + [pl.BlockSpec(memory_space=pltpu.SMEM)] + [in_hbm] * 3,
        out_specs=pl.BlockSpec(memory_space=pltpu.VMEM),
        scratch_shapes=[
            pltpu.VMEM((pieces, n_rows, rhs // pieces, leaf), jnp.bfloat16),
            pltpu.VMEM(far_left.shape[1:], jnp.bfloat16),
            pltpu.VMEM(far_right.shape[1:], jnp.bfloat16),
            pltpu.VMEM(near_blocks.shape[1:], jnp.bfloat16),
            pltpu.VMEM((pieces, rhs // pieces, leaf), jnp.float32),
            pltpu.VMEM((pieces, rhs // pieces, leaf), jnp.float32),
            pltpu.SMEM(far_rows.shape, jnp.int32),
            pltpu.SMEM(far_cols.shape, jnp.int32),
            pltpu.SMEM(far_ranks.shape, jnp.int32),
            pltpu.SMEM(near_rows.shape, jnp.int32),
            pltpu.SMEM(near_cols.shape, jnp.int32),
            pltpu.SemaphoreType.DMA((pieces,)),
            pltpu.SemaphoreType.DMA((3,)),
            pltpu.SemaphoreType.DMA((5,)),
            pltpu.SemaphoreType.DMA((pieces, n_rows)),
            pltpu.SemaphoreType.DMA((pieces, n_rows)),
            pltpu.SemaphoreType.DMA((2, pieces)),
        ],
        compiler_params=pltpu.CompilerParams(
            collective_id=0, has_side_effects=True, vmem_limit_bytes=32 * 1024 * 1024
        ),
    )(*operands)


def solution(mesh):
    split = ("groups", "rows", "cols")
    placed = (
        P(None, split),
        P(split, None, None, None),
        P(split, None, None, None),
        P(split, None),
        P(split, None),
        P(split, None),
        P(split),
        P(split, None, None, None),
        P(split, None),
        P(split, None),
    )
    return jax.shard_map(
        functools.partial(on_device, mesh.shape["rows"], mesh.shape["cols"]),
        mesh=mesh,
        in_specs=placed,
        out_specs=P(None, split),
        check_vma=False,
    )
```
